256 devices in a mesh: row: 16 (over z_hi, x), col: 16 (over y, z_lo, core).
Axes of the slice: x: 4, y: 4, z: 8 (z_hi: 4, z_lo: 2; z = z_hi * 2 + z_lo), core: 2. Of those that a mesh axis runs over, the one named last changes fastest.
Arguments:
- matrix: float32 [16384, 16384], P('row', 'col'), as said below
- reflectors: float32 [5, 64, 16384], P(None, None, 'row'), may hold values from -0.09375 to 0.09375
- factors: float32 [5, 64, 64], replicated, as said below
Outputs:
- updated: float32 [16384, 16384], P('row', 'col')
The draws below stay inside these ranges and needn't reach their ends.
Inputs may be any that keep to these rules, and one draw needn't show every extreme that they name: matrix is symmetric: matrix[r, c] equals matrix[c, r]; its entries are of order one, off the diagonal each the scaled sum of two independent draws of the same law (unbounded normal in one draw, bounded uniform with row and column scales in the other). Each 64 x 64 block of factors is zero below its diagonal.
All inputs are finite; a program needn't handle non-finite values.
Results may differ from the reference program's by a relative error of at most 0.0001.
Values sent between devices are 32-bit elements; how exact they have to be, the bound alone decides.
No kernel may reach another device: no remote copies, remote signals or barrier semaphores. Data moves between devices by JAX's collectives and lax.ppermute only.
A program may use at most 64 MiB of HBM per device.

```python
import jax
import jax.numpy as jnp
from jax import lax

N = 16384
B = 64
PANELS = 5


def draw_matrix(key, part):
    key = jax.random.fold_in(key, 11)
    field_key = jax.random.fold_in(key, 0)
    base_field = jax.random.normal(field_key, (N, N), jnp.float32)
    return (base_field + base_field.T) * 0.7071


def draw_factors(key, part):
    key = jax.random.fold_in(key, 23)
    upper_key, diag_key = jax.random.split(key)
    offdiag = 0.02 * jax.random.normal(upper_key, (PANELS, B, B), jnp.float32)
    diagonal = jax.random.uniform(diag_key, (PANELS, B, B), jnp.float32, 0.45, 0.55)
    index_row = lax.broadcasted_iota(jnp.int32, (PANELS, B, B), 1)
    index_col = lax.broadcasted_iota(jnp.int32, (PANELS, B, B), 2)
    return jnp.where(index_col > index_row, offdiag, 0.0) + jnp.where(index_col == index_row, diagonal, 0.0)


def block_scale(rng, dims, pieces, low, top_value):
    loudness, own = 1.0, jax.random.fold_in(rng, 6)
    for axis_at, parts in pieces:
        steps = jnp.exp(jax.random.uniform(jax.random.fold_in(own, axis_at), (parts,), jnp.float32, low / len(pieces), top_value / len(pieces)))
        loudness = loudness * jnp.repeat(steps, dims[axis_at] // parts).reshape([-1 if axis == axis_at else 1 for axis in range(len(dims))])
    return loudness


def normal_values(own_key, dims, scale, limit, cuts=(), held_as=jnp.bfloat16):
    array = scale * jax.random.normal(own_key, dims, jnp.float32)
    if cuts:
        array = array * block_scale(own_key, dims, cuts, -0.22, 0.18)
    return jnp.clip(array, -limit, limit).astype(held_as)


def setup_inputs(seed: int = 0) -> dict:
    arg_keys = jax.random.split(jax.random.key(seed), 4)
    matrix = draw_matrix(jax.random.fold_in(arg_keys[3], 71), 0)
    reflectors = normal_values(arg_keys[1], (PANELS, B, N), (N // 4) ** -0.5, 0.09375, ((2, 16),), jnp.float32)
    factors = draw_factors(jax.random.fold_in(arg_keys[3], 71), 0)
    return dict(matrix=matrix, reflectors=reflectors, factors=factors)


def contract(former, latter, former_dim, latter_dim):
    return lax.dot_general(former, latter, (((former_dim,), (latter_dim,)), ((), ())), precision=lax.Precision.HIGHEST, preferred_element_type=jnp.float32)


def reference(matrix, reflectors, factors):
    current = matrix
    for panel_index in range(PANELS):
        vectors = reflectors[panel_index]
        factor = factors[panel_index]
        products = contract(vectors, current, 1, 1)
        image_all = contract(factor, products, 0, 0)
        gram_matrix = contract(vectors, image_all, 1, 1)
        shifted = contract(factor, gram_matrix, 0, 0)
        update_all = image_all - 0.5 * contract(shifted, vectors, 0, 0)
        left_side = jnp.concatenate([vectors, update_all], axis=0)
        right_side = jnp.concatenate([update_all, vectors], axis=0)
        current = current - contract(left_side, right_side, 0, 0)
    return current
```

```python
import jax
import jax.numpy as jnp
from jax import lax
from jax.sharding import PartitionSpec as P

HIGH = lax.Precision.HIGH
HIGHEST = lax.Precision.HIGHEST

SHIFT_X = {d: [(i, (i // 4) * 4 + (i + d) % 4) for i in range(16)] for d in (1, 2, 3)}
SHIFT_Z = {d: [(i, (i + 4 * d) % 16) for i in range(16)] for d in (1, 2, 3)}
SHIFT_Y = SHIFT_Z
SWAP_ZLO = [(i, i ^ 2) for i in range(16)]
SWAP_CORE = [(i, i ^ 1) for i in range(16)]
TRANSPOSE = [(r * 16 + c, c * 16 + r) for r in range(16) for c in range(16)]


def dot(a, b, da, db, precision):
    return lax.dot_general(
        a, b, (((da,), (db,)), ((), ())), precision=precision, preferred_element_type=jnp.float32
    )


def piece(a, index, size, dim):
    return lax.dynamic_slice_in_dim(a, index * size, size, dim)


def scatter_sum(a, axis, shifts, index, dim):
    size = a.shape[dim] // 4
    got = [lax.ppermute(piece(a, (index + d) % 4, size, dim), axis, shifts[d]) for d in (2, 1, 3)]
    return piece(a, index, size, dim) + got[0] + got[1] + got[2]


def gather(a, axis, shifts, index, dim):
    size = a.shape[dim]
    got = [(d, lax.ppermute(a, axis, shifts[d])) for d in (2, 1, 3)]
    shape = list(a.shape)
    shape[dim] = 4 * size
    full = lax.dynamic_update_slice_in_dim(jnp.zeros(shape, a.dtype), a, index * size, dim)
    for d, part in got:
        full = lax.dynamic_update_slice_in_dim(full, part, ((index - d) % 4) * size, dim)
    return full


def all_sum(a, axis, shifts):
    got = [lax.ppermute(a, axis, shifts[d]) for d in (2, 1, 3)]
    return a + got[0] + got[1] + got[2]


def swap_gather(a, axis, pairs, index, dim):
    other = lax.ppermute(a, axis, pairs)
    low = jnp.where(index == 0, a, other)
    high = jnp.where(index == 0, other, a)
    return jnp.concatenate([low, high], axis=dim)


def swap_scatter_sum(a, axis, pairs, index, dim):
    size = a.shape[dim] // 2
    other = lax.ppermute(piece(a, 1 - index, size, dim), axis, pairs)
    return piece(a, index, size, dim) + other


def body(matrix, reflectors, factors):
    panels, width, _ = reflectors.shape
    rank = panels * width
    vectors = reflectors.reshape(rank, reflectors.shape[2])
    row, col = lax.axis_index("row"), lax.axis_index("col")
    x, z = row % 4, row // 4
    y, zlo, core = col // 4, (col // 2) % 2, col % 2

    send = piece(piece(vectors, y, 80, 0), col % 4, 256, 1)
    vec_part = lax.ppermute(send, ("row", "col"), TRANSPOSE)

    partial = dot(vectors, matrix, 1, 0, HIGH)
    prod_x = scatter_sum(partial, "row", SHIFT_X, x, 1)
    vec_x = gather(vec_part, "row", SHIFT_Z, z, 0)
    prod_part = scatter_sum(prod_x, "row", SHIFT_Z, z, 0)
    vec_col = gather(vec_x, "row", SHIFT_X, x, 1)

    inner = dot(vec_x, prod_x, 1, 1, HIGH)
    inner = swap_scatter_sum(inner, "col", SWAP_CORE, core, 0)
    inner = scatter_sum(inner, "col", SHIFT_Y, y, 0)
    inner = inner + lax.ppermute(inner, "col", SWAP_ZLO)
    own = piece(piece(vectors, core, rank // 2, 0), y, rank // 8, 0)
    gram = dot(own, vectors, 1, 1, HIGHEST)
    both = jnp.concatenate([inner, gram], axis=0)
    both = all_sum(both, "row", SHIFT_Z)
    both = all_sum(both, "row", SHIFT_X)
    both = both.reshape(2, rank // 8, rank)
    both = gather(both, "col", SHIFT_Y, y, 1)
    both = swap_gather(both, "col", SWAP_CORE, core, 1)
    inner, gram = both[0], both[1]

    factor = factors[0]
    for p in range(1, panels):
        m = p * width
        across = dot(gram[:m, m : m + width], factors[p], 1, 0, HIGHEST)
        top = jnp.concatenate([factor, -dot(factor, across, 1, 0, HIGHEST)], axis=1)
        bottom = jnp.concatenate([jnp.zeros((width, m), jnp.float32), factors[p]], axis=1)
        factor = jnp.concatenate([top, bottom], axis=0)
    middle = dot(factor, dot(inner, factor, 1, 0, HIGHEST), 0, 0, HIGHEST)

    prod_z = gather(prod_part, "row", SHIFT_Z, z, 0)
    prod_col = gather(prod_z, "row", SHIFT_X, x, 1)
    other = lax.ppermute(prod_part, ("row", "col"), TRANSPOSE)
    other = gather(other, "col", SHIFT_Y, y, 0)
    other = swap_gather(other, "col", SWAP_CORE, core, 1)
    prod_row = swap_gather(other, "col", SWAP_ZLO, zlo, 1)

    image_row = dot(factor, prod_row, 0, 0, HIGH)
    image_col = dot(factor, prod_col, 0, 0, HIGH) - dot(middle, vec_col, 0, 0, HIGH)
    left = jnp.concatenate([vectors, image_row], axis=0)
    right = jnp.concatenate([image_col, vec_col], axis=0)
    return matrix - dot(left, right, 0, 0, HIGH)


def solution(mesh):
    in_specs = (P("row", "col"), P(None, None, "row"), P())
    out_specs = P("row", "col")
    return jax.shard_map(body, mesh=mesh, in_specs=in_specs, out_specs=out_specs, check_vma=False)
```

```python
import jax
import jax.numpy as jnp
from jax import lax
from jax.experimental import pallas as pl
from jax.experimental.pallas import tpu as pltpu
from jax.sharding import PartitionSpec as P

HIGH = lax.Precision.HIGH
HIGHEST = lax.Precision.HIGHEST
F32 = jnp.float32
BF16 = jnp.bfloat16
SDS = jax.ShapeDtypeStruct

SHIFT_X = {d: [(i, (i // 4) * 4 + (i + d) % 4) for i in range(16)] for d in (1, 2, 3)}
SHIFT_Z = {d: [(i, (i + 4 * d) % 16) for i in range(16)] for d in (1, 2, 3)}
SHIFT_Y = SHIFT_Z
SWAP_ZLO = [(i, i ^ 2) for i in range(16)]
SWAP_CORE = [(i, i ^ 1) for i in range(16)]
TO_COLUMN = [(c * 16 + 4 * x + z, (z * 4 + x) * 16 + c) for c in range(16) for x in range(4) for z in range(4)]
TO_ROW = [(b, a) for a, b in TO_COLUMN]
EVERYWHERE = ("row", "col")


def flip(bit):
    return [(i, i ^ bit) for i in range(16)]


def dot(a, b, da, db, precision):
    return lax.dot_general(
        a, b, (((da,), (db,)), ((), ())), precision=precision, preferred_element_type=F32
    )


def split(a):
    high = a.astype(BF16)
    return high, (a - high.astype(F32)).astype(BF16)


def wide(a):
    high, low = split(a)
    return jnp.concatenate([high, low, high], axis=1)


def tall(a):
    high, low = split(a)
    return jnp.concatenate([high, high, low], axis=0)


def mul(a, b):
    return jnp.dot(a, b, preferred_element_type=F32)


def dot3(a, b, da, db):
    dims = (((da,), (db,)), ((), ()))
    (ah, al), (bh, bl) = a, b
    out = lax.dot_general(ah, bh, dims, preferred_element_type=F32)
    out += lax.dot_general(ah, bl, dims, preferred_element_type=F32)
    return out + lax.dot_general(al, bh, dims, preferred_element_type=F32)


def piece(a, index, size, dim):
    return lax.dynamic_slice_in_dim(a, index * size, size, dim)


def send(parts, axis, shifts):
    return [lax.ppermute(part, axis, shifts[d]) for d, part in parts]


def whole_kernel(kernel, shapes, place, *operands, scratch=(), flops=0, after=()):
    size = 4 * sum(a.size for a in operands) + sum(s.size * s.dtype.itemsize for s in shapes)
    count = len(operands)
    return pl.pallas_call(
        lambda place, *refs: kernel(place, *refs[:count], *refs[count + len(after) :]),
        out_shape=list(shapes),
        in_specs=[pl.BlockSpec(memory_space=pltpu.SMEM)]
        + [pl.BlockSpec(memory_space=pltpu.VMEM)] * len(operands)
        + [pl.BlockSpec(memory_space=pl.ANY)] * len(after),
        out_specs=[pl.BlockSpec(memory_space=pltpu.VMEM)] * len(shapes),
        scratch_shapes=list(scratch),
        compiler_params=pltpu.CompilerParams(vmem_limit_bytes=40 * 2**20),
        cost_estimate=pl.CostEstimate(flops=flops, bytes_accessed=size, transcendentals=0),
    )(place, *operands, *after)


def at(place_ref, index, size):
    return pl.ds(pl.multiple_of(place_ref[index] * size, size), size)


def quarter_product_kernel(place, vec_ref, mat_ref, *rest):
    outs, turn_ref, vec_split = rest[:4], rest[4], rest[5]
    step = pl.program_id(0)
    rank = vec_ref.shape[0]

    @pl.when(step == 0)
    def _():
        vec_split[:rank], vec_split[rank:] = split(vec_ref[...])
        size, lanes = turn_ref.shape
        turn_ref[...] = vec_ref[at(place, 4, size), at(place, 5, lanes)]

    high, low = split(mat_ref[...])
    both = mul(vec_split[...], high)
    value = both[:rank] + both[rank:] + mul(vec_split[:rank], low)
    for k in range(4):

        @pl.when(step == k)
        def _():
            outs[k][...] = value


def quarter_products(place, vectors, matrix):
    rank, rows = vectors.shape
    width = matrix.shape[1] // 4
    shapes = [SDS((rank, width), F32)] * 4 + [SDS((rank // 4, rows // 4), F32)]
    return pl.pallas_call(
        quarter_product_kernel,
        out_shape=shapes,
        grid_spec=pltpu.PrefetchScalarGridSpec(
            num_scalar_prefetch=1,
            grid=(4,),
            in_specs=[
                pl.BlockSpec((rank, rows), lambda i, place: (0, 0)),
                pl.BlockSpec((rows, width), lambda i, place: (0, place[i])),
            ],
            out_specs=[pl.BlockSpec(s.shape, lambda i, place: (0, 0)) for s in shapes],
            scratch_shapes=[pltpu.VMEM((2 * rank, rows), BF16)],
        ),
        compiler_params=pltpu.CompilerParams(vmem_limit_bytes=40 * 2**20),
        cost_estimate=pl.CostEstimate(
            flops=6 * rank * rows * width * 4,
            bytes_accessed=4 * (rank * rows + rows * width * 4 + rank * width * 4),
            transcendentals=0,
        ),
    )(place, vectors, matrix)


def sum_x_kernel(place, p0, p1, p2, p3, *rest):
    outs, prod_ref = rest[:4], rest[4]
    prod_ref[...] = p0[...] + p1[...] + p2[...] + p3[...]
    for d in range(4):
        outs[d][...] = prod_ref[at(place, d, outs[d].shape[0])]


def sum_z_kernel(place, p0, p1, p2, p3, sum_ref):
    sum_ref[...] = p0[...] + p1[...] + p2[...] + p3[...]


def join_kernel(place, *refs):
    parts, passed, prod_ref, outs = refs[:4], refs[4:6], refs[6], refs[7:]
    for d in range(4):
        prod_ref[at(place, 4 + d, parts[d].shape[0])] = parts[d][...]
    for src_ref, dst_ref in zip(passed, outs):
        dst_ref[...] = src_ref[...]


def inner_kernel(width, place, *refs):
    parts, vecs, vec_ref = refs[:4], refs[4:8], refs[8]
    out_ref, mine_ref, vec_x_ref, prod_ref = refs[9:]
    size, lanes = parts[0].shape
    for d in range(4):
        prod_ref[:, at(place, 2 + d, lanes)] = parts[d][...]
        mine_ref[d] = parts[d][...]
        vec_x_ref[at(place, 6 + d, size)] = vecs[d][...]
    mine = vec_ref[at(place, 0, size)]
    inner = dot(mine, prod_ref[...], 1, 1, HIGHEST)
    gram = dot(mine, vec_ref[at(place, 1, size)], 1, 1, HIGHEST)
    down = (place[0] * size + lax.broadcasted_iota(jnp.int32, inner.shape, 0)) // width
    over = (place[1] * size + lax.broadcasted_iota(jnp.int32, inner.shape, 1)) // width
    out_ref[...] = jnp.where(over >= down, inner, gram)


def sum_kernel(place, a, b, vec_ref, sum_ref, out_ref):
    sum_ref[...] = a[...] + b[...]
    out_ref[...] = vec_ref[...]


def pile_kernel(place, a, b, out_ref):
    out_ref[:2] = a[...]
    out_ref[2:] = b[...]


def factor_kernel(place, mine_ref, other_ref, factors_ref, *rest):
    first_ref, second_ref, factor_ref, strip_ref, both_ref = rest[-5:]
    panels, width, _ = factors_ref.shape
    rank = panels * width
    size = mine_ref.shape[2]
    for k, ref in enumerate((mine_ref, other_ref)):
        for l in range(2):
            for d in range(4):
                strip_ref[place[2 * k + l], at(place, 4 + d, size)] = ref[l, d]
    for q in range(4):
        both_ref[:, q * size : (q + 1) * size] = strip_ref[q]
    both = both_ref[...]
    turned = both.T
    down = lax.broadcasted_iota(jnp.int32, both.shape, 0) // width
    over = lax.broadcasted_iota(jnp.int32, both.shape, 1) // width
    inner = jnp.where(over >= down, both, turned)
    factor_ref[...] = jnp.zeros(factor_ref.shape, F32)
    factor_ref[:width, :width] = factors_ref[0]
    for p in range(1, panels):
        m = p * width
        across = dot(turned[:m, m : m + width], factors_ref[p], 1, 0, HIGHEST)
        factor_ref[:m, m : m + width] = -dot(factor_ref[:m, :m], across, 1, 0, HIGHEST)
        factor_ref[m : m + width, m : m + width] = factors_ref[p]
    factor = factor_ref[...]
    across = factor.T
    middle = mul(wide(across), tall(mul(wide(inner), tall(factor))))
    first_ref[...] = wide(jnp.concatenate([across, -middle], axis=1))
    second_ref[...] = wide(factor)


def left_kernel(place, vec_ref, mine_ref, other_ref, left_ref, prod_ref):
    rank = vec_ref.shape[0]
    for k, ref in enumerate((mine_ref, other_ref)):
        for l in range(2):
            for d in range(4):
                prod_ref[at(place, 2 * k + l, 80), at(place, 4 + d, 256)] = ref[l, d]
    for start, ref in ((0, vec_ref), (rank, prod_ref)):
        high, low = split(ref[...].T)
        left_ref[:, start : start + rank] = high
        left_ref[:, 2 * rank + start : 3 * rank + start] = low
        left_ref[:, 4 * rank + start : 5 * rank + start] = high


def update_kernel(place, *refs):
    prods, vecs = refs[:4], refs[4:8]
    first_ref, second_ref, left_ref, mat_ref, out_ref, new_ref, sems = refs[8:]
    width = prods[0].shape[1]
    copies = []
    for k in range(4):
        prod, vec = prods[k][...], vecs[k][...]
        one = mul(first_ref[...], tall(jnp.concatenate([prod, vec], axis=0)))
        two = mul(second_ref[...], tall(vec))
        right = tall(jnp.concatenate([one, two], axis=0))
        where = at(place, k, width)
        new_ref[:, where] = mat_ref[:, where] - mul(left_ref[...], right)
        copies.append(pltpu.make_async_copy(new_ref.at[:, where], out_ref.at[:, where], sems.at[k]))
        copies[k].start()
    for copy in copies:
        copy.wait()


def update(place, *operands):
    rows, columns = operands[-1].shape
    rank = operands[0].shape[0]
    return pl.pallas_call(
        update_kernel,
        out_shape=SDS((rows, columns), F32),
        in_specs=[pl.BlockSpec(memory_space=pltpu.SMEM)]
        + [pl.BlockSpec(memory_space=pltpu.VMEM)] * len(operands),
        out_specs=pl.BlockSpec(memory_space=pl.ANY),
        scratch_shapes=[pltpu.VMEM((rows, columns), F32), pltpu.SemaphoreType.DMA((4,))],
        compiler_params=pltpu.CompilerParams(vmem_limit_bytes=40 * 2**20),
        cost_estimate=pl.CostEstimate(
            flops=12 * rows * rank * columns, bytes_accessed=8 * rows * columns, transcendentals=0
        ),
    )(place, *operands)


def body(matrix, reflectors, factors):
    panels, width, _ = reflectors.shape
    rank = panels * width
    rows = reflectors.shape[2]
    vectors = reflectors.reshape(rank, rows)
    row, col = lax.axis_index("row"), lax.axis_index("col")
    x, z = row % 4, row // 4
    y, zlo, core = col // 4, (col // 2) % 2, col % 2
    table = lambda entries: jnp.stack(entries).astype(jnp.int32)
    order = [x, (x + 3) % 4, (x + 1) % 4, (x + 2) % 4]
    first = table([(x + 2) % 4, (x + 1) % 4, (x + 3) % 4, x, col % 4, y])
    away = table([(z + d) % 4 for d in range(4)] + [(z - d) % 4 for d in range(4)])
    lanes_at = [(y - d) % 4 for d in range(4)]
    pieces = [2 * (zlo ^ l) + (core ^ k) for k in range(2) for l in range(2)]
    pieces_flip = table(pieces + [y ^ d for d in range(4)])
    pieces_at = table(pieces + lanes_at)
    size, lanes = rank // 4, rows // 4
    slice_shape = SDS((size, lanes), F32)
    quarter_shape = SDS((rank, lanes), F32)
    inner_shape = SDS((size, size), F32)

    with jax.named_scope("products"):
        opposite, right, left, mine, turn = quarter_products(first, vectors, matrix)
    with jax.named_scope("prod_sum_x"):
        got = send([(2, opposite), (1, right), (3, left)], "row", SHIFT_X)
    with jax.named_scope("vec_turn"):
        vec_part = lax.ppermute(turn, EVERYWHERE, TO_COLUMN)
    with jax.named_scope("sum_x"):
        prods = whole_kernel(
            sum_x_kernel, [slice_shape] * 4, away, mine, *got,
            scratch=[pltpu.VMEM(quarter_shape.shape, F32)],
        )
    with jax.named_scope("prod_sum_z"):
        got = send([(d, prods[d]) for d in (2, 1, 3)], "row", SHIFT_Z)
    with jax.named_scope("sum_z"):
        (prod_part,) = whole_kernel(sum_z_kernel, [slice_shape], away, prods[0], *got)
    with jax.named_scope("prod_z"):
        got = send([(d, prod_part) for d in (1, 2, 3)], "row", SHIFT_Z)
    with jax.named_scope("prod_turn"):
        other = lax.ppermute(prod_part, EVERYWHERE, TO_ROW)
    with jax.named_scope("join"):
        prod_z, other, vec_part = whole_kernel(
            join_kernel, [quarter_shape, slice_shape, slice_shape], away, prod_part, *got, other, vec_part
        )
    with jax.named_scope("prod_x"):
        prod_two, prod_left, prod_right = send([(d, prod_z) for d in (2, 1, 3)], "row", SHIFT_X)
    with jax.named_scope("row_y"):
        others = [other] + send([(d, other) for d in (1, 2, 3)], "col", SHIFT_Y)
    with jax.named_scope("vec_z"):
        vecs = [vec_part] + send([(d, vec_part) for d in (1, 2, 3)], "row", SHIFT_Z)
    with jax.named_scope("inner"):
        inner, mine, vec_x = whole_kernel(
            lambda *refs: inner_kernel(width, *refs),
            [inner_shape, SDS((4, size, lanes), F32), quarter_shape],
            table([y, col % 4] + lanes_at + [(z - d) % 4 for d in range(4)]), *others, *vecs, vectors,
            scratch=[pltpu.VMEM((size, rows), F32)], flops=24 * size * size * rows,
            after=[prod_left, prod_right, prod_two],
        )
    with jax.named_scope("row_zlo"):
        mine = jnp.stack([mine, lax.ppermute(mine, "col", SWAP_ZLO)])
    with jax.named_scope("row_core"):
        other = lax.ppermute(mine, "col", SWAP_CORE)
    with jax.named_scope("left"):
        (left,) = whole_kernel(
            left_kernel, [SDS((rows, 6 * rank), BF16)], pieces_at, vectors, mine, other,
            scratch=[pltpu.VMEM((rank, rows), F32)],
        )
    with jax.named_scope("inner_x"):
        inner = inner + lax.ppermute(inner, "row", flip(1))
        got = lax.ppermute(inner, "row", flip(2))
        inner, vec_x = whole_kernel(sum_kernel, [inner_shape, quarter_shape], away, inner, got, vec_x)
    with jax.named_scope("vec_x"):
        vec_two, vec_left, vec_right = send([(d, vec_x) for d in (2, 1, 3)], "row", SHIFT_X)
    with jax.named_scope("inner_z"):
        for d in (4, 8):
            inner = inner + lax.ppermute(inner, "row", flip(d))
    with jax.named_scope("inner_y"):
        inner = jnp.stack([inner, lax.ppermute(inner, "col", flip(4))])
        (inner,) = whole_kernel(
            pile_kernel, [SDS((4, size, size), F32)], away, inner, lax.ppermute(inner, "col", flip(8)),
            after=[left],
        )
    with jax.named_scope("inner_zlo"):
        inner = jnp.stack([inner, lax.ppermute(inner, "col", flip(2))])
    with jax.named_scope("inner_core"):
        inner_other = lax.ppermute(inner, "col", flip(1))
    with jax.named_scope("factor"):
        sides = whole_kernel(
            factor_kernel, [SDS((rank, 6 * rank), BF16), SDS((rank, 3 * rank), BF16)],
            pieces_flip, inner, inner_other, factors,
            scratch=[
                pltpu.VMEM((rank, rank), F32), pltpu.VMEM((4, rank, size), F32), pltpu.VMEM((rank, rank), F32)
            ],
        )
    with jax.named_scope("update"):
        return update(
            table(order), prod_z, prod_left, prod_right, prod_two, vec_x, vec_left, vec_right, vec_two,
            *sides, left, matrix,
        )


def solution(mesh):
    in_specs = (P("row", "col"), P(None, None, "row"), P())
    out_specs = P("row", "col")
    return jax.shard_map(body, mesh=mesh, in_specs=in_specs, out_specs=out_specs, check_vma=False)
```

```python
import jax
import jax.numpy as jnp
from jax import lax
from jax.experimental import pallas as pl
from jax.experimental.pallas import tpu as pltpu
from jax.sharding import PartitionSpec as P

HIGH = lax.Precision.HIGH
HIGHEST = lax.Precision.HIGHEST
F32 = jnp.float32
BF16 = jnp.bfloat16
SDS = jax.ShapeDtypeStruct

SHIFT_X = {d: [(i, (i // 4) * 4 + (i + d) % 4) for i in range(16)] for d in (1, 2, 3)}
SHIFT_Z = {d: [(i, (i + 4 * d) % 16) for i in range(16)] for d in (1, 2, 3)}
SHIFT_Y = SHIFT_Z
SWAP_ZLO = [(i, i ^ 2) for i in range(16)]
SWAP_CORE = [(i, i ^ 1) for i in range(16)]
TO_COLUMN = [(c * 16 + 4 * x + z, (z * 4 + x) * 16 + c) for c in range(16) for x in range(4) for z in range(4)]
TO_ROW = [(b, a) for a, b in TO_COLUMN]
EVERYWHERE = ("row", "col")


def flip(bit):
    return [(i, i ^ bit) for i in range(16)]


def dot(a, b, da, db, precision):
    return lax.dot_general(
        a, b, (((da,), (db,)), ((), ())), precision=precision, preferred_element_type=F32
    )


def split(a):
    high = a.astype(BF16)
    return high, (a - high.astype(F32)).astype(BF16)


def wide(a):
    high, low = split(a)
    return jnp.concatenate([high, low, high], axis=1)


def tall(a):
    high, low = split(a)
    return jnp.concatenate([high, high, low], axis=0)


def mul(a, b):
    return jnp.dot(a, b, preferred_element_type=F32)


def dot3(a, b, da, db):
    dims = (((da,), (db,)), ((), ()))
    (ah, al), (bh, bl) = a, b
    out = lax.dot_general(ah, bh, dims, preferred_element_type=F32)
    out += lax.dot_general(ah, bl, dims, preferred_element_type=F32)
    return out + lax.dot_general(al, bh, dims, preferred_element_type=F32)


def piece(a, index, size, dim):
    return lax.dynamic_slice_in_dim(a, index * size, size, dim)


def send(parts, axis, shifts):
    return [lax.ppermute(part, axis, shifts[d]) for d, part in parts]


def whole_kernel(kernel, shapes, place, *operands, scratch=(), flops=0, after=()):
    size = 4 * sum(a.size for a in operands) + sum(s.size * s.dtype.itemsize for s in shapes)
    count = len(operands)
    return pl.pallas_call(
        lambda place, *refs: kernel(place, *refs[:count], *refs[count + len(after) :]),
        out_shape=list(shapes),
        in_specs=[pl.BlockSpec(memory_space=pltpu.SMEM)]
        + [pl.BlockSpec(memory_space=pltpu.VMEM)] * len(operands)
        + [pl.BlockSpec(memory_space=pl.ANY)] * len(after),
        out_specs=[pl.BlockSpec(memory_space=pltpu.VMEM)] * len(shapes),
        scratch_shapes=list(scratch),
        compiler_params=pltpu.CompilerParams(vmem_limit_bytes=20 * 2**20),
        cost_estimate=pl.CostEstimate(flops=flops, bytes_accessed=size, transcendentals=0),
    )(place, *operands, *after)


def at(place_ref, index, size):
    return pl.ds(pl.multiple_of(place_ref[index] * size, size), size)


def quarter_product_kernel(place, vec_ref, mat_ref, *rest):
    outs, total_ref = rest[:4], rest[4]
    step = pl.program_id(0)
    rank, lanes = outs[0].shape
    vec_high, vec_low = split(vec_ref[...])
    high, low = split(mat_ref[...])
    both = mul(jnp.concatenate([vec_high, vec_low], axis=0), high)
    value = both[:rank] + both[rank:] + mul(vec_high, low)

    @pl.when(step == 0)
    def _():
        total_ref[...] = value

    @pl.when(step > 0)
    def _():
        total_ref[...] += value

    @pl.when(step == pl.num_programs(0) - 1)
    def _():
        for k in range(4):
            outs[k][...] = total_ref[:, at(place, k, lanes)]


def quarter_products(place, vectors, matrix):
    rank, rows = vectors.shape
    columns = matrix.shape[1]
    shape = SDS((rank, columns // 4), F32)
    depth = rows // 4
    return pl.pallas_call(
        quarter_product_kernel,
        out_shape=[shape] * 4,
        grid_spec=pltpu.PrefetchScalarGridSpec(
            num_scalar_prefetch=1,
            grid=(4,),
            in_specs=[
                pl.BlockSpec((rank, depth), lambda i, place: (0, i)),
                pl.BlockSpec((depth, columns), lambda i, place: (i, 0)),
            ],
            out_specs=[pl.BlockSpec(shape.shape, lambda i, place: (0, 0))] * 4,
            scratch_shapes=[pltpu.VMEM((rank, columns), F32)],
        ),
        compiler_params=pltpu.CompilerParams(vmem_limit_bytes=60 * 2**20),
        cost_estimate=pl.CostEstimate(
            flops=6 * rank * rows * rows, bytes_accessed=4 * (2 * rank * rows + rows * rows), transcendentals=0
        ),
    )(place, vectors, matrix)


def sum_x_kernel(place, p0, p1, p2, p3, *rest):
    outs, prod_ref = rest[:4], rest[4]
    prod_ref[...] = p0[...] + p1[...] + p2[...] + p3[...]
    for d in range(4):
        outs[d][...] = prod_ref[at(place, d, outs[d].shape[0])]


def sum_z_kernel(place, p0, p1, p2, p3, vec_ref, pair_ref, sum_ref):
    size = sum_ref.shape[0]
    total = p0[...] + p1[...] + p2[...] + p3[...]
    sum_ref[...] = total
    pair_ref[:size] = total
    pair_ref[size:] = vec_ref[...]


def join_kernel(width, place, *refs):
    (mine, left, right, prod_two, vec_two), other_ref, vec_ref = refs[:5], refs[5], refs[6]
    both_ref, pass_ref, pieces, inner_ref = refs[7], refs[8], refs[9:13], refs[13]
    size, lanes = other_ref.shape
    rank = vec_ref.shape[0]
    for d, (prod, vec) in enumerate(
        ((mine[:size], mine[size:]), (left[:size], left[size:]), (prod_two[...], vec_two[...]),
         (right[:size], right[size:]))
    ):
        both_ref[at(place, d, size)] = prod
        both_ref[at(place, 8 + d, size)] = vec
    pass_ref[...] = other_ref[...]
    here = at(place, 4, lanes)
    vec = split(vec_ref[:, here])
    inner = dot3(vec, split(other_ref[...]), 1, 1)
    gram = dot3(vec, split(vec_ref[at(place, 5, size), here]), 1, 1)
    down = lax.broadcasted_iota(jnp.int32, inner.shape, 0) // width
    over = (place[5] * size + lax.broadcasted_iota(jnp.int32, inner.shape, 1)) // width
    inner_ref[...] = jnp.where(over >= down, inner, gram)
    for d in range(4):
        pieces[d][...] = inner_ref[at(place, 12 + d, size)]


def sum_y_kernel(place, a, b, c, d, p0, p1, p2, p3, sum_ref, mine_ref):
    sum_ref[...] = a[...] + b[...] + c[...] + d[...]
    for d, part in enumerate((p0, p1, p2, p3)):
        mine_ref[d] = part[...]


def add_z_kernel(place, a, b, c, d, mine, other, left_ref, right_ref, sum_ref, both_ref, prod_ref, vec_ref):
    rank = prod_ref.shape[0]
    sum_ref[...] = a[...] + b[...] + c[...] + d[...]
    both_ref[0] = mine[...]
    both_ref[1] = other[...]
    prod_ref[...] = left_ref[:rank]
    vec_ref[...] = right_ref[rank:]


def add_x_kernel(place, a, b, c, d, prod_ref, vec_ref, sum_ref, prod_out, vec_out):
    sum_ref[...] = a[...] + b[...] + c[...] + d[...]
    prod_out[...] = prod_ref[...]
    vec_out[...] = vec_ref[...]


def factor_kernel(place, mine_ref, other_ref, factors_ref, *rest):
    first_ref, second_ref, factor_ref, strip_ref, both_ref = rest
    panels, width, _ = factors_ref.shape
    rank = panels * width
    size = mine_ref.shape[2]
    for k, ref in enumerate((mine_ref, other_ref)):
        for l in range(2):
            for d in range(4):
                strip_ref[place[2 * k + l], at(place, 4 + d, size)] = ref[l, d]
    for q in range(4):
        both_ref[:, q * size : (q + 1) * size] = strip_ref[q]
    both = both_ref[...]
    turned = both.T
    down = lax.broadcasted_iota(jnp.int32, both.shape, 0) // width
    over = lax.broadcasted_iota(jnp.int32, both.shape, 1) // width
    inner = jnp.where(over >= down, both, turned)
    factor_ref[...] = jnp.zeros(factor_ref.shape, F32)
    factor_ref[:width, :width] = factors_ref[0]
    for p in range(1, panels):
        m = p * width
        across = dot(turned[:m, m : m + width], factors_ref[p], 1, 0, HIGHEST)
        factor_ref[:m, m : m + width] = -dot(factor_ref[:m, :m], across, 1, 0, HIGHEST)
        factor_ref[m : m + width, m : m + width] = factors_ref[p]
    factor = factor_ref[...]
    across = factor.T
    middle = mul(wide(across), tall(mul(wide(inner), tall(factor))))
    first_ref[...] = wide(jnp.concatenate([across, -middle], axis=1))
    second_ref[...] = wide(factor)


def left_kernel(place, vec_ref, mine_ref, other_ref, left_ref, prod_ref):
    rank = vec_ref.shape[0]
    for k, ref in enumerate((mine_ref, other_ref)):
        for l in range(2):
            for d in range(4):
                prod_ref[at(place, 2 * k + l, 80), at(place, 4 + d, 256)] = ref[l, d]
    for start, ref in ((0, vec_ref), (rank, prod_ref)):
        high, low = split(ref[...].T)
        left_ref[:, start : start + rank] = high
        left_ref[:, 2 * rank + start : 3 * rank + start] = low
        left_ref[:, 4 * rank + start : 5 * rank + start] = high


def update_kernel(place, *refs):
    near, (prod_two, vec_two) = refs[:3], refs[3:5]
    first_ref, second_ref, left_ref, mat_ref, out_ref, new_ref, sems = refs[5:]
    rank, width = prod_two.shape
    copies = []
    for k in range(4):
        if k < 3:
            prod, vec = near[k][:rank], near[k][rank:]
        else:
            prod, vec = prod_two[...], vec_two[...]
        one = mul(first_ref[...], tall(jnp.concatenate([prod, vec], axis=0)))
        two = mul(second_ref[...], tall(vec))
        right = tall(jnp.concatenate([one, two], axis=0))
        where = at(place, k, width)
        new_ref[:, where] = mat_ref[:, where] - mul(left_ref[...], right)
        copies.append(pltpu.make_async_copy(new_ref.at[:, where], out_ref.at[:, where], sems.at[k]))
        copies[k].start()
    for copy in copies:
        copy.wait()


def update(place, *operands):
    rows, columns = operands[-1].shape
    rank = operands[0].shape[0] // 2
    return pl.pallas_call(
        update_kernel,
        out_shape=SDS((rows, columns), F32),
        in_specs=[pl.BlockSpec(memory_space=pltpu.SMEM)]
        + [pl.BlockSpec(memory_space=pltpu.VMEM)] * len(operands),
        out_specs=pl.BlockSpec(memory_space=pl.ANY),
        scratch_shapes=[pltpu.VMEM((rows, columns), F32), pltpu.SemaphoreType.DMA((4,))],
        compiler_params=pltpu.CompilerParams(vmem_limit_bytes=20 * 2**20),
        cost_estimate=pl.CostEstimate(
            flops=12 * rows * rank * columns, bytes_accessed=8 * rows * columns, transcendentals=0
        ),
    )(place, *operands)


def body(matrix, reflectors, factors):
    panels, width, _ = reflectors.shape
    rank = panels * width
    rows = reflectors.shape[2]
    vectors = reflectors.reshape(rank, rows)
    row, col = lax.axis_index("row"), lax.axis_index("col")
    x, z = row % 4, row // 4
    y, zlo, core = col // 4, (col // 2) % 2, col % 2
    table = lambda entries: jnp.stack(entries).astype(jnp.int32)
    order = [x, (x + 3) % 4, (x + 1) % 4, (x + 2) % 4]
    first = table([(x + 2) % 4, (x + 1) % 4, (x + 3) % 4, x, col % 4, y])
    from_z = [(z - d) % 4 for d in range(4)]
    away = table([(z + d) % 4 for d in range(4)] + from_z)
    lanes_at = [(y - d) % 4 for d in range(4)]
    pieces_at = table([2 * (zlo ^ l) + (core ^ k) for k in range(2) for l in range(2)] + lanes_at)
    size, lanes = rank // 4, rows // 4
    slice_shape = SDS((size, lanes), F32)
    quarter_shape = SDS((rank, lanes), F32)
    inner_shape = SDS((size, size), F32)

    with jax.named_scope("vec_turn"):
        turn = piece(piece(vectors, col % 4, size, 0), y, lanes, 1)
        vec_part = lax.ppermute(turn, EVERYWHERE, TO_COLUMN)
    with jax.named_scope("products"):
        opposite, right, left, mine = quarter_products(first, vectors, matrix)
    with jax.named_scope("prod_sum_x"):
        got = send([(2, opposite), (1, right), (3, left)], "row", SHIFT_X)
    with jax.named_scope("sum_x"):
        prods = whole_kernel(
            sum_x_kernel, [slice_shape] * 4, away, mine, *got,
            scratch=[pltpu.VMEM(quarter_shape.shape, F32)],
        )
    with jax.named_scope("prod_sum_z"):
        got = send([(d, prods[d]) for d in (1, 2, 3)], "row", SHIFT_Z)
    with jax.named_scope("sum_z"):
        pair, prod_part = whole_kernel(
            sum_z_kernel, [SDS((2 * size, lanes), F32), slice_shape], away, prods[0], *got, vec_part
        )
    with jax.named_scope("prod_turn"):
        other = lax.ppermute(prod_part, EVERYWHERE, TO_ROW)
    with jax.named_scope("pair_z"):
        left, right = send([(1, pair), (3, pair)], "row", SHIFT_Z)
        two = send([(1, left[:size]), (3, right[size:])], "row", SHIFT_Z)
    with jax.named_scope("join"):
        pair, other, *inners = whole_kernel(
            lambda *refs: join_kernel(width, *refs),
            [SDS((2 * rank, lanes), F32), slice_shape] + [inner_shape] * 4,
            table(
                from_z + [y, col % 4, y, y] + [4 + i for i in from_z] + [(y + d) % 4 for d in range(4)]
            ),
            pair, left, right, *two, other, vectors,
            scratch=[pltpu.VMEM((rank, size), F32)], flops=24 * rank * size * lanes,
        )
    with jax.named_scope("pair_x"):
        pair_left, pair_right = send([(1, pair), (3, pair)], "row", SHIFT_X)
    with jax.named_scope("row_y"):
        others = [other] + send([(d, other) for d in (1, 2, 3)], "col", SHIFT_Y)
    with jax.named_scope("inner_y"):
        got = send([(d, inners[d]) for d in (1, 2, 3)], "col", SHIFT_Y)
        inner, mine = whole_kernel(
            sum_y_kernel, [inner_shape, SDS((4, size, lanes), F32)], away, inners[0], *got, *others
        )
    with jax.named_scope("row_zlo"):
        other = lax.ppermute(mine, "col", SWAP_ZLO)
    with jax.named_scope("inner_z"):
        got = send([(d, inner) for d in (1, 2, 3)], "row", SHIFT_Z)
        inner, mine, *two = whole_kernel(
            add_z_kernel, [inner_shape, SDS((2, 4, size, lanes), F32), quarter_shape, quarter_shape],
            away, inner, *got, mine, other, pair_left, pair_right,
        )
    with jax.named_scope("row_core"):
        other = lax.ppermute(mine, "col", SWAP_CORE)
    with jax.named_scope("inner_x"):
        got = send([(d, inner) for d in (1, 2, 3)], "row", SHIFT_X)
        inner, *two = whole_kernel(
            add_x_kernel, [inner_shape, quarter_shape, quarter_shape], away, inner, *got, *two, after=[other]
        )
    with jax.named_scope("pair_two"):
        two = [lax.ppermute(two[0], "row", SHIFT_X[1]), lax.ppermute(two[1], "row", SHIFT_X[3])]
    with jax.named_scope("inner_gy"):
        inner = jnp.stack([inner] + send([(d, inner) for d in (1, 2, 3)], "col", SHIFT_Y))
    with jax.named_scope("inner_zlo"):
        inner = jnp.stack([inner, lax.ppermute(inner, "col", SWAP_ZLO)])
    with jax.named_scope("inner_core"):
        inner_other = lax.ppermute(inner, "col", SWAP_CORE)
    with jax.named_scope("left"):
        (left,) = whole_kernel(
            left_kernel, [SDS((rows, 6 * rank), BF16)], pieces_at, vectors, mine, other,
            scratch=[pltpu.VMEM((rank, rows), F32)], after=[inner_other],
        )
    with jax.named_scope("factor"):
        sides = whole_kernel(
            factor_kernel, [SDS((rank, 6 * rank), BF16), SDS((rank, 3 * rank), BF16)],
            pieces_at, inner, inner_other, factors,
            scratch=[
                pltpu.VMEM((rank, rank), F32), pltpu.VMEM((4, rank, size), F32), pltpu.VMEM((rank, rank), F32)
            ],
            after=two,
        )
    with jax.named_scope("update"):
        return update(table(order), pair, pair_left, pair_right, *two, *sides, left, matrix)


def solution(mesh):
    in_specs = (P("row", "col"), P(None, None, "row"), P())
    out_specs = P("row", "col")
    return jax.shard_map(body, mesh=mesh, in_specs=in_specs, out_specs=out_specs, check_vma=False)
```

```python
import jax
import jax.numpy as jnp
from jax import lax
from jax.experimental import pallas as pl
from jax.experimental.pallas import tpu as pltpu
from jax.sharding import PartitionSpec as P

HIGH = lax.Precision.HIGH
HIGHEST = lax.Precision.HIGHEST
F32 = jnp.float32
BF16 = jnp.bfloat16
SDS = jax.ShapeDtypeStruct

SHIFT_X = {d: [(i, (i // 4) * 4 + (i + d) % 4) for i in range(16)] for d in (1, 2, 3)}
SHIFT_Z = {d: [(i, (i + 4 * d) % 16) for i in range(16)] for d in (1, 2, 3)}
SHIFT_Y = SHIFT_Z
SWAP_ZLO = [(i, i ^ 2) for i in range(16)]
SWAP_CORE = [(i, i ^ 1) for i in range(16)]
TO_COLUMN = [(c * 16 + 4 * x + z, (z * 4 + x) * 16 + c) for c in range(16) for x in range(4) for z in range(4)]
TO_ROW = [(b, a) for a, b in TO_COLUMN]
EVERYWHERE = ("row", "col")


def flip(bit):
    return [(i, i ^ bit) for i in range(16)]


def dot(a, b, da, db, precision):
    return lax.dot_general(
        a, b, (((da,), (db,)), ((), ())), precision=precision, preferred_element_type=F32
    )


def split(a):
    high = a.astype(BF16)
    return high, (a - high.astype(F32)).astype(BF16)


def wide(a):
    high, low = split(a)
    return jnp.concatenate([high, low, high], axis=1)


def tall(a):
    high, low = split(a)
    return jnp.concatenate([high, high, low], axis=0)


def mul(a, b):
    return jnp.dot(a, b, preferred_element_type=F32)


def dot3(a, b, da, db):
    dims = (((da,), (db,)), ((), ()))
    (ah, al), (bh, bl) = a, b
    out = lax.dot_general(ah, bh, dims, preferred_element_type=F32)
    out += lax.dot_general(ah, bl, dims, preferred_element_type=F32)
    return out + lax.dot_general(al, bh, dims, preferred_element_type=F32)


def piece(a, index, size, dim):
    return lax.dynamic_slice_in_dim(a, index * size, size, dim)


def send(parts, axis, shifts):
    return [lax.ppermute(part, axis, shifts[d]) for d, part in parts]


def whole_kernel(kernel, shapes, place, *operands, scratch=(), flops=0, after=()):
    size = 4 * sum(a.size for a in operands) + sum(s.size * s.dtype.itemsize for s in shapes)
    count = len(operands)
    return pl.pallas_call(
        lambda place, *refs: kernel(place, *refs[:count], *refs[count + len(after) :]),
        out_shape=list(shapes),
        in_specs=[pl.BlockSpec(memory_space=pltpu.SMEM)]
        + [pl.BlockSpec(memory_space=pltpu.VMEM)] * len(operands)
        + [pl.BlockSpec(memory_space=pl.ANY)] * len(after),
        out_specs=[pl.BlockSpec(memory_space=pltpu.VMEM)] * len(shapes),
        scratch_shapes=list(scratch),
        compiler_params=pltpu.CompilerParams(vmem_limit_bytes=20 * 2**20),
        cost_estimate=pl.CostEstimate(flops=flops, bytes_accessed=size, transcendentals=0),
    )(place, *operands, *after)


def tie(a, *after):
    return pl.pallas_call(
        lambda *refs: None,
        out_shape=SDS(a.shape, a.dtype),
        in_specs=[pl.BlockSpec(memory_space=pl.ANY)] * (1 + len(after)),
        out_specs=pl.BlockSpec(memory_space=pl.ANY),
        input_output_aliases={0: 0},
    )(a, *after)


def at(place_ref, index, size):
    return pl.ds(pl.multiple_of(place_ref[index] * size, size), size)


def quarter_product_kernel(vec_ref, mat_ref, *rest):
    outs, total_ref = rest[:4], rest[4]
    step = pl.program_id(0)
    rank, lanes = outs[0].shape
    value = mul(wide(vec_ref[...]), tall(mat_ref[...]))

    @pl.when(step == 0)
    def _():
        total_ref[...] = value

    @pl.when(step > 0)
    def _():
        total_ref[...] += value

    @pl.when(step == pl.num_programs(0) - 1)
    def _():
        x = lax.rem(lax.axis_index("row"), 4)
        for out, d in zip(outs, (2, 1, 3, 0)):
            start = pl.multiple_of(lax.rem(x + d, 4) * lanes, lanes)
            out[...] = total_ref[:, pl.ds(start, lanes)]


def quarter_products(vectors, matrix):
    rank, rows = vectors.shape
    columns = matrix.shape[1]
    shape = SDS((rank, columns // 4), F32)
    depth = rows // 4
    return pl.pallas_call(
        quarter_product_kernel,
        out_shape=[shape] * 4,
        grid=(4,),
        in_specs=[
            pl.BlockSpec((rank, depth), lambda i: (0, i)),
            pl.BlockSpec((depth, columns), lambda i: (i, 0)),
        ],
        out_specs=[pl.BlockSpec(shape.shape, lambda i: (0, 0))] * 4,
        scratch_shapes=[pltpu.VMEM((rank, columns), F32)],
        compiler_params=pltpu.CompilerParams(vmem_limit_bytes=60 * 2**20),
        cost_estimate=pl.CostEstimate(
            flops=6 * rank * rows * rows, bytes_accessed=4 * (2 * rank * rows + rows * rows), transcendentals=0
        ),
    )(vectors, matrix)


def sum_x_kernel(place, p0, p1, p2, p3, *rest):
    outs, prod_ref = rest[:4], rest[4]
    prod_ref[...] = p0[...] + p1[...] + p2[...] + p3[...]
    for d in range(4):
        outs[d][...] = prod_ref[at(place, d, outs[d].shape[0])]


def sum_z_kernel(place, p0, p1, p2, p3, vec_ref, pair_ref, sum_ref):
    size = sum_ref.shape[0]
    total = p0[...] + p1[...] + p2[...] + p3[...]
    sum_ref[...] = total
    pair_ref[:size] = total
    pair_ref[size:] = vec_ref[...]


def join_kernel(width, place, *refs):
    (mine, left, right, prod_two, vec_two), other_ref, vec_ref = refs[:5], refs[5], refs[6]
    both_ref, pass_ref, pieces, inner_ref = refs[7], refs[8], refs[9:13], refs[13]
    size, lanes = other_ref.shape
    rank = vec_ref.shape[0]
    for d, (prod, vec) in enumerate(
        ((mine[:size], mine[size:]), (left[:size], left[size:]), (prod_two[...], vec_two[...]),
         (right[:size], right[size:]))
    ):
        both_ref[at(place, d, size)] = prod
        both_ref[at(place, 8 + d, size)] = vec
    pass_ref[...] = other_ref[...]
    here = at(place, 4, lanes)
    vec = split(vec_ref[:, here])
    inner = dot3(vec, split(other_ref[...]), 1, 1)
    gram = dot3(vec, split(vec_ref[at(place, 5, size), here]), 1, 1)
    down = lax.broadcasted_iota(jnp.int32, inner.shape, 0) // width
    over = (place[5] * size + lax.broadcasted_iota(jnp.int32, inner.shape, 1)) // width
    inner_ref[...] = jnp.where(over >= down, inner, gram)
    for d in range(4):
        pieces[d][...] = inner_ref[at(place, 12 + d, size)]


def sum_y_kernel(place, a, b, c, d, p0, p1, p2, p3, sum_ref, mine_ref):
    sum_ref[...] = a[...] + b[...] + c[...] + d[...]
    for d, part in enumerate((p0, p1, p2, p3)):
        mine_ref[d] = part[...]


def add_z_kernel(place, a, b, c, d, mine, other, left_ref, right_ref, sum_ref, both_ref, prod_ref, vec_ref):
    rank = prod_ref.shape[0]
    sum_ref[...] = a[...] + b[...] + c[...] + d[...]
    both_ref[0] = mine[...]
    both_ref[1] = other[...]
    prod_ref[...] = left_ref[:rank]
    vec_ref[...] = right_ref[rank:]


def add_x_kernel(place, a, b, c, d, prod_ref, vec_ref, sum_ref, prod_out, vec_out):
    sum_ref[...] = a[...] + b[...] + c[...] + d[...]
    prod_out[...] = prod_ref[...]
    vec_out[...] = vec_ref[...]


def factor_kernel(place, mine_ref, other_ref, factors_ref, *rest):
    first_ref, second_ref, factor_ref, strip_ref, both_ref = rest
    panels, width, _ = factors_ref.shape
    rank = panels * width
    size = mine_ref.shape[2]
    for k, ref in enumerate((mine_ref, other_ref)):
        for l in range(2):
            for d in range(4):
                strip_ref[place[2 * k + l], at(place, 4 + d, size)] = ref[l, d]
    for q in range(4):
        both_ref[:, q * size : (q + 1) * size] = strip_ref[q]
    both = both_ref[...]
    turned = both.T
    down = lax.broadcasted_iota(jnp.int32, both.shape, 0) // width
    over = lax.broadcasted_iota(jnp.int32, both.shape, 1) // width
    inner = jnp.where(over >= down, both, turned)
    factor_ref[...] = jnp.zeros(factor_ref.shape, F32)
    factor_ref[:width, :width] = factors_ref[0]
    for p in range(1, panels):
        m = p * width
        across = dot(turned[:m, m : m + width], factors_ref[p], 1, 0, HIGHEST)
        factor_ref[:m, m : m + width] = -dot(factor_ref[:m, :m], across, 1, 0, HIGHEST)
        factor_ref[m : m + width, m : m + width] = factors_ref[p]
    factor = factor_ref[...]
    across = factor.T
    middle = mul(wide(across), tall(mul(wide(inner), tall(factor))))
    first_ref[...] = wide(jnp.concatenate([across, -middle], axis=1))
    second_ref[...] = wide(factor)


def left_kernel(place, vec_ref, mine_ref, other_ref, left_ref, prod_ref):
    rank = vec_ref.shape[0]
    for k, ref in enumerate((mine_ref, other_ref)):
        for l in range(2):
            for d in range(4):
                prod_ref[at(place, 2 * k + l, 80), at(place, 4 + d, 256)] = ref[l, d]
    for start, ref in ((0, vec_ref), (rank, prod_ref)):
        high, low = split(ref[...].T)
        left_ref[:, start : start + rank] = high
        left_ref[:, 2 * rank + start : 3 * rank + start] = low
        left_ref[:, 4 * rank + start : 5 * rank + start] = high


def update_kernel(place, *refs):
    near, (prod_two, vec_two) = refs[:3], refs[3:5]
    first_ref, second_ref, left_ref, mat_ref, out_ref, new_ref, right_ref, sems = refs[5:]
    rank, width = prod_two.shape
    step = 256
    copies = []
    for half in range(2):
        if half == 0:
            pair = jnp.concatenate([near[0][...], near[1][...]], axis=1)
        else:
            far = jnp.concatenate([prod_two[...], vec_two[...]], axis=0)
            pair = jnp.concatenate([near[2][...], far], axis=1)
        one = mul(first_ref[...], tall(pair))
        two = mul(second_ref[...], tall(pair[rank:]))
        right_ref[...] = tall(jnp.concatenate([one, two], axis=0))
        for m in range(mat_ref.shape[0] // step):
            rows = pl.ds(m * step, step)
            change = mul(left_ref[rows], right_ref[...])
            for j in range(2):
                where = at(place, 2 * half + j, width)
                new_ref[rows, where] = mat_ref[rows, where] - change[:, j * width : (j + 1) * width]
                copy = pltpu.make_async_copy(
                    new_ref.at[rows, where], out_ref.at[rows, where], sems.at[len(copies)]
                )
                copy.start()
                copies.append(copy)
    for copy in copies:
        copy.wait()


def update(place, *operands):
    rows, columns = operands[-1].shape
    rank = operands[0].shape[0] // 2
    return pl.pallas_call(
        update_kernel,
        out_shape=SDS((rows, columns), F32),
        in_specs=[pl.BlockSpec(memory_space=pltpu.SMEM)]
        + [pl.BlockSpec(memory_space=pltpu.VMEM)] * len(operands),
        out_specs=pl.BlockSpec(memory_space=pl.ANY),
        scratch_shapes=[
            pltpu.VMEM((rows, columns), F32),
            pltpu.VMEM((6 * rank, columns // 2), BF16),
            pltpu.SemaphoreType.DMA((16,)),
        ],
        compiler_params=pltpu.CompilerParams(vmem_limit_bytes=20 * 2**20),
        cost_estimate=pl.CostEstimate(
            flops=12 * rows * rank * columns, bytes_accessed=8 * rows * columns, transcendentals=0
        ),
    )(place, *operands)


def body(matrix, reflectors, factors):
    panels, width, _ = reflectors.shape
    rank = panels * width
    rows = reflectors.shape[2]
    vectors = reflectors.reshape(rank, rows)
    row, col = lax.axis_index("row"), lax.axis_index("col")
    x, z = row % 4, row // 4
    y, zlo, core = col // 4, (col // 2) % 2, col % 2
    table = lambda entries: jnp.stack(entries).astype(jnp.int32)
    order = [x, (x + 3) % 4, (x + 1) % 4, (x + 2) % 4]
    from_z = [(z - d) % 4 for d in range(4)]
    away = table([(z + d) % 4 for d in range(4)] + from_z)
    lanes_at = [(y - d) % 4 for d in range(4)]
    pieces_at = table([2 * (zlo ^ l) + (core ^ k) for k in range(2) for l in range(2)] + lanes_at)
    size, lanes = rank // 4, rows // 4
    slice_shape = SDS((size, lanes), F32)
    quarter_shape = SDS((rank, lanes), F32)
    inner_shape = SDS((size, size), F32)

    with jax.named_scope("products"):
        opposite, right, left, mine = quarter_products(vectors, matrix)
    with jax.named_scope("prod_sum_x"):
        got = send([(2, opposite), (1, right), (3, left)], "row", SHIFT_X)
    with jax.named_scope("vec_turn"):
        turn = piece(piece(vectors, col % 4, size, 0), y, lanes, 1)
        vec_part = lax.ppermute(tie(turn, got[0][:8, :128]), EVERYWHERE, TO_COLUMN)
    with jax.named_scope("sum_x"):
        prods = whole_kernel(
            sum_x_kernel, [slice_shape] * 4, away, mine, *got,
            scratch=[pltpu.VMEM(quarter_shape.shape, F32)],
        )
    with jax.named_scope("prod_sum_z"):
        got = send([(d, prods[d]) for d in (1, 2, 3)], "row", SHIFT_Z)
    with jax.named_scope("sum_z"):
        pair, prod_part = whole_kernel(
            sum_z_kernel, [SDS((2 * size, lanes), F32), slice_shape], away, prods[0], *got, vec_part
        )
    with jax.named_scope("prod_turn"):
        other = lax.ppermute(prod_part, EVERYWHERE, TO_ROW)
    with jax.named_scope("pair_z"):
        left, right = send([(1, pair), (3, pair)], "row", SHIFT_Z)
        two = send([(1, left[:size]), (3, right[size:])], "row", SHIFT_Z)
    with jax.named_scope("join"):
        pair, other, *inners = whole_kernel(
            lambda *refs: join_kernel(width, *refs),
            [SDS((2 * rank, lanes), F32), slice_shape] + [inner_shape] * 4,
            table(
                from_z + [y, col % 4, y, y] + [4 + i for i in from_z] + [(y + d) % 4 for d in range(4)]
            ),
            pair, left, right, *two, other, vectors,
            scratch=[pltpu.VMEM((rank, size), F32)], flops=24 * rank * size * lanes,
        )
    with jax.named_scope("pair_x"):
        pair_left, pair_right = send([(1, pair), (3, pair)], "row", SHIFT_X)
    with jax.named_scope("row_y"):
        others = [other] + send([(d, other) for d in (1, 2, 3)], "col", SHIFT_Y)
    with jax.named_scope("inner_y"):
        got = send([(d, inners[d]) for d in (1, 2, 3)], "col", SHIFT_Y)
        inner, mine = whole_kernel(
            sum_y_kernel, [inner_shape, SDS((4, size, lanes), F32)], away, inners[0], *got, *others
        )
    with jax.named_scope("row_zlo"):
        other = lax.ppermute(mine, "col", SWAP_ZLO)
    with jax.named_scope("inner_z"):
        got = send([(d, inner) for d in (1, 2, 3)], "row", SHIFT_Z)
        inner, mine, *two = whole_kernel(
            add_z_kernel, [inner_shape, SDS((2, 4, size, lanes), F32), quarter_shape, quarter_shape],
            away, inner, *got, mine, other, pair_left, pair_right,
        )
    with jax.named_scope("row_core"):
        other = lax.ppermute(mine, "col", SWAP_CORE)
    with jax.named_scope("inner_x"):
        got = send([(d, inner) for d in (1, 2, 3)], "row", SHIFT_X)
        inner, *two = whole_kernel(
            add_x_kernel, [inner_shape, quarter_shape, quarter_shape], away, inner, *got, *two, after=[other]
        )
    with jax.named_scope("pair_two"):
        two = [lax.ppermute(two[0], "row", SHIFT_X[1]), lax.ppermute(two[1], "row", SHIFT_X[3])]
    with jax.named_scope("inner_gy"):
        inner = jnp.stack([inner] + send([(d, inner) for d in (1, 2, 3)], "col", SHIFT_Y))
    with jax.named_scope("inner_zlo"):
        inner = jnp.stack([inner, lax.ppermute(inner, "col", SWAP_ZLO)])
    with jax.named_scope("inner_core"):
        inner_other = lax.ppermute(inner, "col", SWAP_CORE)
    with jax.named_scope("left"):
        (left,) = whole_kernel(
            left_kernel, [SDS((rows, 6 * rank), BF16)], pieces_at, vectors, mine, other,
            scratch=[pltpu.VMEM((rank, rows), F32)], after=[inner_other],
        )
    with jax.named_scope("factor"):
        sides = whole_kernel(
            factor_kernel, [SDS((rank, 6 * rank), BF16), SDS((rank, 3 * rank), BF16)],
            pieces_at, inner, inner_other, factors,
            scratch=[
                pltpu.VMEM((rank, rank), F32), pltpu.VMEM((4, rank, size), F32), pltpu.VMEM((rank, rank), F32)
            ],
            after=two,
        )
    with jax.named_scope("update"):
        return update(table(order), pair, pair_left, pair_right, *two, *sides, left, matrix)


def solution(mesh):
    in_specs = (P("row", "col"), P(None, None, "row"), P())
    out_specs = P("row", "col")
    return jax.shard_map(body, mesh=mesh, in_specs=in_specs, out_specs=out_specs, check_vma=False)
```

```python
import jax
import jax.numpy as jnp
from jax import lax
from jax.experimental import pallas as pl
from jax.experimental.pallas import tpu as pltpu
from jax.sharding import PartitionSpec as P

HIGH = lax.Precision.HIGH
HIGHEST = lax.Precision.HIGHEST
F32 = jnp.float32
BF16 = jnp.bfloat16
SDS = jax.ShapeDtypeStruct

SHIFT_X = {d: [(i, (i // 4) * 4 + (i + d) % 4) for i in range(16)] for d in (1, 2, 3)}
SHIFT_Z = {d: [(i, (i + 4 * d) % 16) for i in range(16)] for d in (1, 2, 3)}
SHIFT_Y = SHIFT_Z
SWAP_ZLO = [(i, i ^ 2) for i in range(16)]
SWAP_CORE = [(i, i ^ 1) for i in range(16)]
TO_COLUMN = [(c * 16 + 4 * x + z, (z * 4 + x) * 16 + c) for c in range(16) for x in range(4) for z in range(4)]
TO_ROW = [(b, a) for a, b in TO_COLUMN]
EVERYWHERE = ("row", "col")


def flip(bit):
    return [(i, i ^ bit) for i in range(16)]


def dot(a, b, da, db, precision):
    return lax.dot_general(
        a, b, (((da,), (db,)), ((), ())), precision=precision, preferred_element_type=F32
    )


def split(a):
    high = a.astype(BF16)
    return high, (a - high.astype(F32)).astype(BF16)


def wide(a):
    high, low = split(a)
    return jnp.concatenate([high, low, high], axis=1)


def tall(a):
    high, low = split(a)
    return jnp.concatenate([high, high, low], axis=0)


def mul(a, b):
    return jnp.dot(a, b, preferred_element_type=F32)


def dot3(a, b, da, db):
    dims = (((da,), (db,)), ((), ()))
    (ah, al), (bh, bl) = a, b
    out = lax.dot_general(ah, bh, dims, preferred_element_type=F32)
    out += lax.dot_general(ah, bl, dims, preferred_element_type=F32)
    return out + lax.dot_general(al, bh, dims, preferred_element_type=F32)


def piece(a, index, size, dim):
    return lax.dynamic_slice_in_dim(a, index * size, size, dim)


def send(parts, axis, shifts):
    return [lax.ppermute(part, axis, shifts[d]) for d, part in parts]


def whole_kernel(kernel, shapes, place, *operands, scratch=(), flops=0, after=()):
    size = 4 * sum(a.size for a in operands) + sum(s.size * s.dtype.itemsize for s in shapes)
    count = len(operands)
    return pl.pallas_call(
        lambda place, *refs: kernel(place, *refs[:count], *refs[count + len(after) :]),
        out_shape=list(shapes),
        in_specs=[pl.BlockSpec(memory_space=pltpu.SMEM)]
        + [pl.BlockSpec(memory_space=pltpu.VMEM)] * len(operands)
        + [pl.BlockSpec(memory_space=pl.ANY)] * len(after),
        out_specs=[pl.BlockSpec(memory_space=pltpu.VMEM)] * len(shapes),
        scratch_shapes=list(scratch),
        compiler_params=pltpu.CompilerParams(vmem_limit_bytes=20 * 2**20),
        cost_estimate=pl.CostEstimate(flops=flops, bytes_accessed=size, transcendentals=0),
    )(place, *operands, *after)


def tie(a, *after):
    return pl.pallas_call(
        lambda *refs: None,
        out_shape=SDS(a.shape, a.dtype),
        in_specs=[pl.BlockSpec(memory_space=pl.ANY)] * (1 + len(after)),
        out_specs=pl.BlockSpec(memory_space=pl.ANY),
        input_output_aliases={0: 0},
    )(a, *after)


def at(place_ref, index, size):
    return pl.ds(pl.multiple_of(place_ref[index] * size, size), size)


def quarter_product_kernel(vec_ref, mat_ref, *rest):
    outs, total_ref = rest[:4], rest[4]
    step = pl.program_id(0)
    rank, lanes = outs[0].shape
    value = mul(wide(vec_ref[...]), tall(mat_ref[...]))

    @pl.when(step == 0)
    def _():
        total_ref[...] = value

    @pl.when(step > 0)
    def _():
        total_ref[...] += value

    @pl.when(step == pl.num_programs(0) - 1)
    def _():
        x = lax.rem(lax.axis_index("row"), 4)
        for out, d in zip(outs, (2, 1, 3, 0)):
            start = pl.multiple_of(lax.rem(x + d, 4) * lanes, lanes)
            out[...] = total_ref[:, pl.ds(start, lanes)]


def quarter_products(vectors, matrix):
    rank, rows = vectors.shape
    columns = matrix.shape[1]
    shape = SDS((rank, columns // 4), F32)
    depth = rows // 4
    return pl.pallas_call(
        quarter_product_kernel,
        out_shape=[shape] * 4,
        grid=(4,),
        in_specs=[
            pl.BlockSpec((rank, depth), lambda i: (0, i)),
            pl.BlockSpec((depth, columns), lambda i: (i, 0)),
        ],
        out_specs=[pl.BlockSpec(shape.shape, lambda i: (0, 0))] * 4,
        scratch_shapes=[pltpu.VMEM((rank, columns), F32)],
        compiler_params=pltpu.CompilerParams(vmem_limit_bytes=60 * 2**20),
        cost_estimate=pl.CostEstimate(
            flops=6 * rank * rows * rows, bytes_accessed=4 * (2 * rank * rows + rows * rows), transcendentals=0
        ),
    )(vectors, matrix)


def sum_x_kernel(place, p0, p1, p2, p3, *rest):
    outs, prod_ref = rest[:4], rest[4]
    prod_ref[...] = p0[...] + p1[...] + p2[...] + p3[...]
    for d in range(4):
        outs[d][...] = prod_ref[at(place, d, outs[d].shape[0])]


def sum_z_kernel(place, p0, p1, p2, p3, vec_ref, pair_ref, sum_ref):
    size = sum_ref.shape[0]
    total = p0[...] + p1[...] + p2[...] + p3[...]
    sum_ref[...] = total
    pair_ref[:size] = total
    pair_ref[size:] = vec_ref[...]


def join_kernel(width, place, *refs):
    (mine, left, right, prod_two, vec_two), other_ref, vec_ref = refs[:5], refs[5], refs[6]
    both_ref, pass_ref, pieces, inner_ref = refs[7], refs[8], refs[9:13], refs[13]
    size, lanes = other_ref.shape
    rank = vec_ref.shape[0]
    for d, (prod, vec) in enumerate(
        ((mine[:size], mine[size:]), (left[:size], left[size:]), (prod_two[...], vec_two[...]),
         (right[:size], right[size:]))
    ):
        both_ref[at(place, d, size)] = prod
        both_ref[at(place, 8 + d, size)] = vec
    pass_ref[...] = other_ref[...]
    here = at(place, 4, lanes)
    vec = split(vec_ref[:, here])
    inner = dot3(vec, split(other_ref[...]), 1, 1)
    gram = dot3(vec, split(vec_ref[at(place, 5, size), here]), 1, 1)
    down = lax.broadcasted_iota(jnp.int32, inner.shape, 0) // width
    over = (place[5] * size + lax.broadcasted_iota(jnp.int32, inner.shape, 1)) // width
    inner_ref[...] = jnp.where(over >= down, inner, gram)
    for d in range(4):
        pieces[d][...] = inner_ref[at(place, 12 + d, size)]


def sum_y_kernel(place, a, b, c, d, p0, p1, p2, p3, sum_ref, mine_ref):
    sum_ref[...] = a[...] + b[...] + c[...] + d[...]
    for d, part in enumerate((p0, p1, p2, p3)):
        mine_ref[d] = part[...]


def add_z_kernel(place, a, b, c, d, mine, left_ref, right_ref, sum_ref, pass_ref, prod_ref, vec_ref):
    rank = prod_ref.shape[0]
    sum_ref[...] = a[...] + b[...] + c[...] + d[...]
    pass_ref[...] = mine[...]
    prod_ref[...] = left_ref[:rank]
    vec_ref[...] = right_ref[rank:]


def add_x_kernel(place, a, b, c, d, mine, other, prod_ref, vec_ref, sum_ref, both_ref, prod_out, vec_out):
    sum_ref[...] = a[...] + b[...] + c[...] + d[...]
    both_ref[0] = mine[...]
    both_ref[1] = other[...]
    prod_out[...] = prod_ref[...]
    vec_out[...] = vec_ref[...]


def factor_kernel(place, mine_ref, other_ref, factors_ref, *rest):
    first_ref, second_ref, factor_ref, strip_ref, both_ref = rest
    panels, width, _ = factors_ref.shape
    rank = panels * width
    size = mine_ref.shape[2]
    for k, ref in enumerate((mine_ref, other_ref)):
        for l in range(2):
            for d in range(4):
                strip_ref[place[2 * k + l], at(place, 4 + d, size)] = ref[l, d]
    for q in range(4):
        both_ref[:, q * size : (q + 1) * size] = strip_ref[q]
    both = both_ref[...]
    turned = both.T
    down = lax.broadcasted_iota(jnp.int32, both.shape, 0) // width
    over = lax.broadcasted_iota(jnp.int32, both.shape, 1) // width
    inner = jnp.where(over >= down, both, turned)
    factor_ref[...] = jnp.zeros(factor_ref.shape, F32)
    factor_ref[:width, :width] = factors_ref[0]
    for p in range(1, panels):
        m = p * width
        across = dot(turned[:m, m : m + width], factors_ref[p], 1, 0, HIGHEST)
        factor_ref[:m, m : m + width] = -dot(factor_ref[:m, :m], across, 1, 0, HIGHEST)
        factor_ref[m : m + width, m : m + width] = factors_ref[p]
    factor = factor_ref[...]
    across = factor.T
    middle = mul(wide(across), tall(mul(wide(inner), tall(factor))))
    first_ref[...] = wide(jnp.concatenate([across, -middle], axis=1))
    second_ref[...] = wide(factor)


def left_kernel(place, vec_ref, mine_ref, other_ref, left_ref, prod_ref):
    rank = vec_ref.shape[0]
    for k, ref in enumerate((mine_ref, other_ref)):
        for l in range(2):
            for d in range(4):
                prod_ref[at(place, 2 * k + l, 80), at(place, 4 + d, 256)] = ref[l, d]
    for start, ref in ((0, vec_ref), (rank, prod_ref)):
        high, low = split(ref[...].T)
        left_ref[:, start : start + rank] = high
        left_ref[:, 2 * rank + start : 3 * rank + start] = low
        left_ref[:, 4 * rank + start : 5 * rank + start] = high


def update_kernel(place, *refs):
    near, (prod_two, vec_two) = refs[:3], refs[3:5]
    first_ref, second_ref, left_ref, mat_ref, out_ref, new_ref, right_ref, sems = refs[5:]
    rank, width = prod_two.shape
    step = 256
    copies = []
    for half in range(2):
        if half == 0:
            pair = jnp.concatenate([near[0][...], near[1][...]], axis=1)
        else:
            far = jnp.concatenate([prod_two[...], vec_two[...]], axis=0)
            pair = jnp.concatenate([near[2][...], far], axis=1)
        one = mul(first_ref[...], tall(pair))
        two = mul(second_ref[...], tall(pair[rank:]))
        right_ref[...] = tall(jnp.concatenate([one, two], axis=0))
        for m in range(mat_ref.shape[0] // step):
            rows = pl.ds(m * step, step)
            change = mul(left_ref[rows], right_ref[...])
            for j in range(2):
                where = at(place, 2 * half + j, width)
                new_ref[rows, where] = mat_ref[rows, where] - change[:, j * width : (j + 1) * width]
                copy = pltpu.make_async_copy(
                    new_ref.at[rows, where], out_ref.at[rows, where], sems.at[len(copies)]
                )
                copy.start()
                copies.append(copy)
    for copy in copies:
        copy.wait()


def update(place, *operands):
    rows, columns = operands[-1].shape
    rank = operands[0].shape[0] // 2
    return pl.pallas_call(
        update_kernel,
        out_shape=SDS((rows, columns), F32),
        in_specs=[pl.BlockSpec(memory_space=pltpu.SMEM)]
        + [pl.BlockSpec(memory_space=pltpu.VMEM)] * len(operands),
        out_specs=pl.BlockSpec(memory_space=pl.ANY),
        scratch_shapes=[
            pltpu.VMEM((rows, columns), F32),
            pltpu.VMEM((6 * rank, columns // 2), BF16),
            pltpu.SemaphoreType.DMA((16,)),
        ],
        compiler_params=pltpu.CompilerParams(vmem_limit_bytes=20 * 2**20),
        cost_estimate=pl.CostEstimate(
            flops=12 * rows * rank * columns, bytes_accessed=8 * rows * columns, transcendentals=0
        ),
    )(place, *operands)


def body(matrix, reflectors, factors):
    panels, width, _ = reflectors.shape
    rank = panels * width
    rows = reflectors.shape[2]
    vectors = reflectors.reshape(rank, rows)
    row, col = lax.axis_index("row"), lax.axis_index("col")
    x, z = row % 4, row // 4
    y, zlo, core = col // 4, (col // 2) % 2, col % 2
    table = lambda entries: jnp.stack(entries).astype(jnp.int32)
    order = [x, (x + 3) % 4, (x + 1) % 4, (x + 2) % 4]
    from_z = [(z - d) % 4 for d in range(4)]
    away = table([(z + d) % 4 for d in range(4)] + from_z)
    lanes_at = [(y - d) % 4 for d in range(4)]
    pieces_at = table([2 * (zlo ^ l) + (core ^ k) for k in range(2) for l in range(2)] + lanes_at)
    size, lanes = rank // 4, rows // 4
    slice_shape = SDS((size, lanes), F32)
    quarter_shape = SDS((rank, lanes), F32)
    inner_shape = SDS((size, size), F32)

    with jax.named_scope("products"):
        opposite, right, left, mine = quarter_products(vectors, matrix)
    with jax.named_scope("prod_sum_x"):
        got = send([(2, opposite), (1, right), (3, left)], "row", SHIFT_X)
    with jax.named_scope("vec_turn"):
        turn = piece(piece(vectors, col % 4, size, 0), y, lanes, 1)
        vec_part = lax.ppermute(tie(turn, got[0][:8, :128]), EVERYWHERE, TO_COLUMN)
    with jax.named_scope("sum_x"):
        prods = whole_kernel(
            sum_x_kernel, [slice_shape] * 4, away, mine, *got,
            scratch=[pltpu.VMEM(quarter_shape.shape, F32)],
        )
    with jax.named_scope("prod_sum_z"):
        got = send([(d, prods[d]) for d in (1, 2, 3)], "row", SHIFT_Z)
    with jax.named_scope("sum_z"):
        pair, prod_part = whole_kernel(
            sum_z_kernel, [SDS((2 * size, lanes), F32), slice_shape], away, prods[0], *got, vec_part
        )
    with jax.named_scope("prod_turn"):
        other = lax.ppermute(prod_part, EVERYWHERE, TO_ROW)
    with jax.named_scope("pair_z"):
        left, right = send([(1, pair), (3, pair)], "row", SHIFT_Z)
        two = send([(1, left[:size]), (3, right[size:])], "row", SHIFT_Z)
    with jax.named_scope("join"):
        pair, other, *inners = whole_kernel(
            lambda *refs: join_kernel(width, *refs),
            [SDS((2 * rank, lanes), F32), slice_shape] + [inner_shape] * 4,
            table(
                from_z + [y, col % 4, y, y] + [4 + i for i in from_z] + [(y + d) % 4 for d in range(4)]
            ),
            pair, left, right, *two, other, vectors,
            scratch=[pltpu.VMEM((rank, size), F32)], flops=24 * rank * size * lanes,
        )
    with jax.named_scope("pair_x"):
        pair_left, pair_right = send([(1, pair), (3, pair)], "row", SHIFT_X)
    with jax.named_scope("row_y"):
        others = [other] + send([(d, other) for d in (1, 2, 3)], "col", SHIFT_Y)
    with jax.named_scope("inner_y"):
        got = send([(d, inners[d]) for d in (1, 2, 3)], "col", SHIFT_Y)
        inner, mine = whole_kernel(
            sum_y_kernel, [inner_shape, SDS((4, size, lanes), F32)], away, inners[0], *got, *others
        )
    with jax.named_scope("inner_z"):
        got = send([(d, inner) for d in (1, 2, 3)], "row", SHIFT_Z)
        inner, mine, *two = whole_kernel(
            add_z_kernel, [inner_shape, SDS((4, size, lanes), F32), quarter_shape, quarter_shape],
            away, inner, *got, mine, pair_left, pair_right,
        )
    with jax.named_scope("row_zlo"):
        other = lax.ppermute(mine, "col", SWAP_ZLO)
    with jax.named_scope("inner_x"):
        got = send([(d, inner) for d in (1, 2, 3)], "row", SHIFT_X)
        inner, mine, *two = whole_kernel(
            add_x_kernel, [inner_shape, SDS((2, 4, size, lanes), F32), quarter_shape, quarter_shape],
            away, inner, *got, mine, other, *two,
        )
    with jax.named_scope("row_core"):
        other = lax.ppermute(mine, "col", SWAP_CORE)
    with jax.named_scope("pair_two"):
        two = [lax.ppermute(two[0], "row", SHIFT_X[1]), lax.ppermute(two[1], "row", SHIFT_X[3])]
    with jax.named_scope("inner_gy"):
        inner = jnp.stack([inner] + send([(d, inner) for d in (1, 2, 3)], "col", SHIFT_Y))
    with jax.named_scope("inner_zlo"):
        inner = jnp.stack([inner, lax.ppermute(inner, "col", SWAP_ZLO)])
    with jax.named_scope("inner_core"):
        inner_other = lax.ppermute(inner, "col", SWAP_CORE)
    with jax.named_scope("left"):
        (left,) = whole_kernel(
            left_kernel, [SDS((rows, 6 * rank), BF16)], pieces_at, vectors, mine, other,
            scratch=[pltpu.VMEM((rank, rows), F32)], after=[inner],
        )
    with jax.named_scope("factor"):
        sides = whole_kernel(
            factor_kernel, [SDS((rank, 6 * rank), BF16), SDS((rank, 3 * rank), BF16)],
            pieces_at, inner, inner_other, factors,
            scratch=[
                pltpu.VMEM((rank, rank), F32), pltpu.VMEM((4, rank, size), F32), pltpu.VMEM((rank, rank), F32)
            ],
            after=[*two, left],
        )
    with jax.named_scope("update"):
        return update(table(order), pair, pair_left, pair_right, *two, *sides, left, matrix)


def solution(mesh):
    in_specs = (P("row", "col"), P(None, None, "row"), P())
    out_specs = P("row", "col")
    return jax.shard_map(body, mesh=mesh, in_specs=in_specs, out_specs=out_specs, check_vma=False)
```

```python
import jax
import jax.numpy as jnp
from jax import lax
from jax.experimental import pallas as pl
from jax.experimental.pallas import tpu as pltpu
from jax.sharding import PartitionSpec as P

HIGH = lax.Precision.HIGH
HIGHEST = lax.Precision.HIGHEST
F32 = jnp.float32
BF16 = jnp.bfloat16
SDS = jax.ShapeDtypeStruct

SHIFT_X = {d: [(i, (i // 4) * 4 + (i + d) % 4) for i in range(16)] for d in (1, 2, 3)}
SHIFT_Z = {d: [(i, (i + 4 * d) % 16) for i in range(16)] for d in (1, 2, 3)}
SHIFT_Y = SHIFT_Z
SWAP_ZLO = [(i, i ^ 2) for i in range(16)]
SWAP_CORE = [(i, i ^ 1) for i in range(16)]
TO_COLUMN = [(c * 16 + 4 * x + z, (z * 4 + x) * 16 + c) for c in range(16) for x in range(4) for z in range(4)]
TO_ROW = [(b, a) for a, b in TO_COLUMN]
EVERYWHERE = ("row", "col")


def flip(bit):
    return [(i, i ^ bit) for i in range(16)]


def dot(a, b, da, db, precision):
    return lax.dot_general(
        a, b, (((da,), (db,)), ((), ())), precision=precision, preferred_element_type=F32
    )


def split(a):
    high = a.astype(BF16)
    return high, (a - high.astype(F32)).astype(BF16)


def wide(a):
    high, low = split(a)
    return jnp.concatenate([high, low, high], axis=1)


def tall(a):
    high, low = split(a)
    return jnp.concatenate([high, high, low], axis=0)


def mul(a, b):
    return jnp.dot(a, b, preferred_element_type=F32)


def dot3(a, b, da, db):
    dims = (((da,), (db,)), ((), ()))
    (ah, al), (bh, bl) = a, b
    out = lax.dot_general(ah, bh, dims, preferred_element_type=F32)
    out += lax.dot_general(ah, bl, dims, preferred_element_type=F32)
    return out + lax.dot_general(al, bh, dims, preferred_element_type=F32)


def piece(a, index, size, dim):
    return lax.dynamic_slice_in_dim(a, index * size, size, dim)


def send(parts, axis, shifts):
    return [lax.ppermute(part, axis, shifts[d]) for d, part in parts]


def whole_kernel(kernel, shapes, place, *operands, scratch=(), flops=0, after=()):
    size = 4 * sum(a.size for a in operands) + sum(s.size * s.dtype.itemsize for s in shapes)
    count = len(operands)
    return pl.pallas_call(
        lambda place, *refs: kernel(place, *refs[:count], *refs[count + len(after) :]),
        out_shape=list(shapes),
        in_specs=[pl.BlockSpec(memory_space=pltpu.SMEM)]
        + [pl.BlockSpec(memory_space=pltpu.VMEM)] * len(operands)
        + [pl.BlockSpec(memory_space=pl.ANY)] * len(after),
        out_specs=[pl.BlockSpec(memory_space=pltpu.VMEM)] * len(shapes),
        scratch_shapes=list(scratch),
        compiler_params=pltpu.CompilerParams(vmem_limit_bytes=20 * 2**20),
        cost_estimate=pl.CostEstimate(flops=flops, bytes_accessed=size, transcendentals=0),
    )(place, *operands, *after)


def tie(a, *after):
    return pl.pallas_call(
        lambda *refs: None,
        out_shape=SDS(a.shape, a.dtype),
        in_specs=[pl.BlockSpec(memory_space=pl.ANY)] * (1 + len(after)),
        out_specs=pl.BlockSpec(memory_space=pl.ANY),
        input_output_aliases={0: 0},
    )(a, *after)


def at(place_ref, index, size):
    return pl.ds(pl.multiple_of(place_ref[index] * size, size), size)


def quarter_product_kernel(vec_ref, mat_ref, *rest):
    outs, total_ref = rest[:4], rest[4]
    step = pl.program_id(0)
    rank, lanes = outs[0].shape
    value = mul(wide(vec_ref[...]), tall(mat_ref[...]))

    @pl.when(step == 0)
    def _():
        total_ref[...] = value

    @pl.when(step > 0)
    def _():
        total_ref[...] += value

    @pl.when(step == pl.num_programs(0) - 1)
    def _():
        x = lax.rem(lax.axis_index("row"), 4)
        for out, d in zip(outs, (2, 1, 3, 0)):
            start = pl.multiple_of(lax.rem(x + d, 4) * lanes, lanes)
            out[...] = total_ref[:, pl.ds(start, lanes)]


def quarter_products(vectors, matrix):
    rank, rows = vectors.shape
    columns = matrix.shape[1]
    shape = SDS((rank, columns // 4), F32)
    depth = rows // 4
    return pl.pallas_call(
        quarter_product_kernel,
        out_shape=[shape] * 4,
        grid=(4,),
        in_specs=[
            pl.BlockSpec((rank, depth), lambda i: (0, i)),
            pl.BlockSpec((depth, columns), lambda i: (i, 0)),
        ],
        out_specs=[pl.BlockSpec(shape.shape, lambda i: (0, 0))] * 4,
        scratch_shapes=[pltpu.VMEM((rank, columns), F32)],
        compiler_params=pltpu.CompilerParams(vmem_limit_bytes=60 * 2**20),
        cost_estimate=pl.CostEstimate(
            flops=6 * rank * rows * rows, bytes_accessed=4 * (2 * rank * rows + rows * rows), transcendentals=0
        ),
    )(vectors, matrix)


def sum_x_kernel(place, p0, p1, p2, p3, *rest):
    outs, prod_ref = rest[:4], rest[4]
    prod_ref[...] = p0[...] + p1[...] + p2[...] + p3[...]
    for d in range(4):
        outs[d][...] = prod_ref[at(place, d, outs[d].shape[0])]


def sum_z_kernel(place, p0, p1, p2, p3, vec_ref, pair_ref, sum_ref):
    size = sum_ref.shape[0]
    total = p0[...] + p1[...] + p2[...] + p3[...]
    sum_ref[...] = total
    pair_ref[:size] = total
    pair_ref[size:] = vec_ref[...]


def join_kernel(width, place, *refs):
    (mine, left, right, prod_two, vec_two), other_ref, vec_ref = refs[:5], refs[5], refs[6]
    both_ref, pass_ref, pieces, inner_ref = refs[7], refs[8], refs[9:13], refs[13]
    size, lanes = other_ref.shape
    rank = vec_ref.shape[0]
    for d, (prod, vec) in enumerate(
        ((mine[:size], mine[size:]), (left[:size], left[size:]), (prod_two[...], vec_two[...]),
         (right[:size], right[size:]))
    ):
        both_ref[at(place, d, size)] = prod
        both_ref[at(place, 8 + d, size)] = vec
    pass_ref[...] = other_ref[...]
    here = at(place, 4, lanes)
    vec = split(vec_ref[:, here])
    inner = dot3(vec, split(other_ref[...]), 1, 1)
    gram = dot3(vec, split(vec_ref[at(place, 5, size), here]), 1, 1)
    down = lax.broadcasted_iota(jnp.int32, inner.shape, 0) // width
    over = (place[5] * size + lax.broadcasted_iota(jnp.int32, inner.shape, 1)) // width
    inner_ref[...] = jnp.where(over >= down, inner, gram)
    for d in range(4):
        pieces[d][...] = inner_ref[at(place, 12 + d, size)]


def sum_y_kernel(place, a, b, c, d, p0, p1, p2, p3, sum_ref, mine_ref):
    sum_ref[...] = a[...] + b[...] + c[...] + d[...]
    for d, part in enumerate((p0, p1, p2, p3)):
        mine_ref[d] = part[...]


def add_z_kernel(place, a, b, c, d, mine, left_ref, right_ref, sum_ref, pass_ref, prod_ref, vec_ref):
    rank = prod_ref.shape[0]
    sum_ref[...] = a[...] + b[...] + c[...] + d[...]
    pass_ref[...] = mine[...]
    prod_ref[...] = left_ref[:rank]
    vec_ref[...] = right_ref[rank:]


def add_x_kernel(place, a, b, c, d, mine, other, prod_ref, vec_ref, sum_ref, both_ref, prod_out, vec_out):
    sum_ref[...] = a[...] + b[...] + c[...] + d[...]
    both_ref[0] = mine[...]
    both_ref[1] = other[...]
    prod_out[...] = prod_ref[...]
    vec_out[...] = vec_ref[...]


def factor_kernel(place, mine_ref, other_ref, factors_ref, *rest):
    first_ref, second_ref, factor_ref, strip_ref, both_ref = rest
    panels, width, _ = factors_ref.shape
    rank = panels * width
    size = mine_ref.shape[2]
    for k, ref in enumerate((mine_ref, other_ref)):
        for l in range(2):
            for d in range(4):
                strip_ref[place[2 * k + l], at(place, 4 + d, size)] = ref[l, d]
    for q in range(4):
        both_ref[:, q * size : (q + 1) * size] = strip_ref[q]
    both = both_ref[...]
    turned = both.T
    down = lax.broadcasted_iota(jnp.int32, both.shape, 0) // width
    over = lax.broadcasted_iota(jnp.int32, both.shape, 1) // width
    inner = jnp.where(over >= down, both, turned)
    factor_ref[...] = jnp.zeros(factor_ref.shape, F32)
    factor_ref[:width, :width] = factors_ref[0]
    for p in range(1, panels):
        m = p * width
        across = dot(turned[:m, m : m + width], factors_ref[p], 1, 0, HIGHEST)
        factor_ref[:m, m : m + width] = -dot(factor_ref[:m, :m], across, 1, 0, HIGHEST)
        factor_ref[m : m + width, m : m + width] = factors_ref[p]
    factor = factor_ref[...]
    across = factor.T
    middle = mul(wide(across), tall(mul(wide(inner), tall(factor))))
    first_ref[...] = wide(jnp.concatenate([across, -middle], axis=1))
    second_ref[...] = wide(factor)


def left_kernel(place, vec_ref, mine_ref, other_ref, left_ref, prod_ref):
    rank = vec_ref.shape[0]
    for k, ref in enumerate((mine_ref, other_ref)):
        for l in range(2):
            for d in range(4):
                prod_ref[at(place, 2 * k + l, 80), at(place, 4 + d, 256)] = ref[l, d]
    for start, ref in ((0, vec_ref), (rank, prod_ref)):
        high, low = split(ref[...].T)
        left_ref[:, start : start + rank] = high
        left_ref[:, 2 * rank + start : 3 * rank + start] = low
        left_ref[:, 4 * rank + start : 5 * rank + start] = high


def update_kernel(place, *refs):
    near, (prod_two, vec_two) = refs[:3], refs[3:5]
    first_ref, second_ref, left_ref, mat_ref, out_ref, new_ref, right_ref, sems = refs[5:]
    rank, width = prod_two.shape
    step = 256
    copies = []
    for half in range(2):
        if half == 0:
            pair = jnp.concatenate([near[0][...], near[1][...]], axis=1)
        else:
            far = jnp.concatenate([prod_two[...], vec_two[...]], axis=0)
            pair = jnp.concatenate([near[2][...], far], axis=1)
        one = mul(first_ref[...], tall(pair))
        two = mul(second_ref[...], tall(pair[rank:]))
        right_ref[...] = tall(jnp.concatenate([one, two], axis=0))
        for m in range(mat_ref.shape[0] // step):
            rows = pl.ds(m * step, step)
            change = mul(left_ref[rows], right_ref[...])
            for j in range(2):
                where = at(place, 2 * half + j, width)
                new_ref[rows, where] = mat_ref[rows, where] - change[:, j * width : (j + 1) * width]
                copy = pltpu.make_async_copy(
                    new_ref.at[rows, where], out_ref.at[rows, where], sems.at[len(copies)]
                )
                copy.start()
                copies.append(copy)
    for copy in copies:
        copy.wait()


def update(place, *operands):
    rows, columns = operands[-1].shape
    rank = operands[0].shape[0] // 2
    return pl.pallas_call(
        update_kernel,
        out_shape=SDS((rows, columns), F32),
        in_specs=[pl.BlockSpec(memory_space=pltpu.SMEM)]
        + [pl.BlockSpec(memory_space=pltpu.VMEM)] * len(operands),
        out_specs=pl.BlockSpec(memory_space=pl.ANY),
        scratch_shapes=[
            pltpu.VMEM((rows, columns), F32),
            pltpu.VMEM((6 * rank, columns // 2), BF16),
            pltpu.SemaphoreType.DMA((16,)),
        ],
        compiler_params=pltpu.CompilerParams(vmem_limit_bytes=20 * 2**20),
        cost_estimate=pl.CostEstimate(
            flops=12 * rows * rank * columns, bytes_accessed=8 * rows * columns, transcendentals=0
        ),
    )(place, *operands)


def body(matrix, reflectors, factors):
    panels, width, _ = reflectors.shape
    rank = panels * width
    rows = reflectors.shape[2]
    vectors = reflectors.reshape(rank, rows)
    row, col = lax.axis_index("row"), lax.axis_index("col")
    x, z = row % 4, row // 4
    y, zlo, core = col // 4, (col // 2) % 2, col % 2
    table = lambda entries: jnp.stack(entries).astype(jnp.int32)
    order = [x, (x + 3) % 4, (x + 1) % 4, (x + 2) % 4]
    from_z = [(z - d) % 4 for d in range(4)]
    away = table([(z + d) % 4 for d in range(4)] + from_z)
    lanes_at = [(y - d) % 4 for d in range(4)]
    pieces_at = table([2 * (zlo ^ l) + (core ^ k) for k in range(2) for l in range(2)] + lanes_at)
    size, lanes = rank // 4, rows // 4
    slice_shape = SDS((size, lanes), F32)
    quarter_shape = SDS((rank, lanes), F32)
    inner_shape = SDS((size, size), F32)

    with jax.named_scope("products"):
        opposite, right, left, mine = quarter_products(vectors, matrix)
    with jax.named_scope("prod_sum_x"):
        got = send([(2, opposite), (1, right), (3, left)], "row", SHIFT_X)
    with jax.named_scope("vec_turn"):
        turn = piece(piece(vectors, col % 4, size, 0), y, lanes, 1)
        vec_part = lax.ppermute(tie(turn, got[0][:8, :128]), EVERYWHERE, TO_COLUMN)
    with jax.named_scope("sum_x"):
        prods = whole_kernel(
            sum_x_kernel, [slice_shape] * 4, away, mine, *got,
            scratch=[pltpu.VMEM(quarter_shape.shape, F32)],
        )
    with jax.named_scope("prod_sum_z"):
        got = send([(d, prods[d]) for d in (1, 2, 3)], "row", SHIFT_Z)
    with jax.named_scope("sum_z"):
        pair, prod_part = whole_kernel(
            sum_z_kernel, [SDS((2 * size, lanes), F32), slice_shape], away, prods[0], *got, vec_part
        )
    with jax.named_scope("prod_turn"):
        other = lax.ppermute(prod_part, EVERYWHERE, TO_ROW)
    with jax.named_scope("pair_z"):
        left, right = send([(1, pair), (3, pair)], "row", SHIFT_Z)
        two = send([(1, left[:size]), (3, right[size:])], "row", SHIFT_Z)
    with jax.named_scope("join"):
        pair, other, *inners = whole_kernel(
            lambda *refs: join_kernel(width, *refs),
            [SDS((2 * rank, lanes), F32), slice_shape] + [inner_shape] * 4,
            table(
                from_z + [y, col % 4, y, y] + [4 + i for i in from_z] + [(y + d) % 4 for d in range(4)]
            ),
            pair, left, right, *two, other, vectors,
            scratch=[pltpu.VMEM((rank, size), F32)], flops=24 * rank * size * lanes,
        )
    with jax.named_scope("pair_x"):
        pair_left, pair_right = send([(1, pair), (3, pair)], "row", SHIFT_X)
    with jax.named_scope("row_y"):
        others = [other] + send([(d, other) for d in (1, 2, 3)], "col", SHIFT_Y)
    with jax.named_scope("inner_y"):
        got = send([(d, inners[d]) for d in (1, 2, 3)], "col", SHIFT_Y)
        inner, mine = whole_kernel(
            sum_y_kernel, [inner_shape, SDS((4, size, lanes), F32)], away, inners[0], *got, *others
        )
    with jax.named_scope("inner_z"):
        got = send([(d, inner) for d in (1, 2, 3)], "row", SHIFT_Z)
        inner, mine, *two = whole_kernel(
            add_z_kernel, [inner_shape, SDS((4, size, lanes), F32), quarter_shape, quarter_shape],
            away, inner, *got, mine, pair_left, pair_right,
        )
    with jax.named_scope("row_zlo"):
        other = lax.ppermute(mine, "col", SWAP_ZLO)
    with jax.named_scope("inner_x"):
        got = send([(d, inner) for d in (1, 2, 3)], "row", SHIFT_X)
        inner, mine, *two = whole_kernel(
            add_x_kernel, [inner_shape, SDS((2, 4, size, lanes), F32), quarter_shape, quarter_shape],
            away, inner, *got, mine, other, *two,
        )
    with jax.named_scope("pair_two"):
        two = [lax.ppermute(two[0], "row", SHIFT_X[1]), lax.ppermute(two[1], "row", SHIFT_X[3])]
    with jax.named_scope("inner_gy"):
        got = send([(d, inner) for d in (1, 2, 3)], "col", SHIFT_Y)
        inner = jnp.stack([inner] + got)
    with jax.named_scope("row_core"):
        mine = tie(mine, *got)
        other = lax.ppermute(mine, "col", SWAP_CORE)
    with jax.named_scope("inner_zlo"):
        inner = jnp.stack([inner, lax.ppermute(inner, "col", SWAP_ZLO)])
    with jax.named_scope("inner_core"):
        inner_other = lax.ppermute(inner, "col", SWAP_CORE)
    with jax.named_scope("left"):
        (left,) = whole_kernel(
            left_kernel, [SDS((rows, 6 * rank), BF16)], pieces_at, vectors, mine, other,
            scratch=[pltpu.VMEM((rank, rows), F32)], after=[inner],
        )
    with jax.named_scope("factor"):
        sides = whole_kernel(
            factor_kernel, [SDS((rank, 6 * rank), BF16), SDS((rank, 3 * rank), BF16)],
            pieces_at, inner, inner_other, factors,
            scratch=[
                pltpu.VMEM((rank, rank), F32), pltpu.VMEM((4, rank, size), F32), pltpu.VMEM((rank, rank), F32)
            ],
            after=[*two, left],
        )
    with jax.named_scope("update"):
        return update(table(order), pair, pair_left, pair_right, *two, *sides, left, matrix)


def solution(mesh):
    in_specs = (P("row", "col"), P(None, None, "row"), P())
    out_specs = P("row", "col")
    return jax.shard_map(body, mesh=mesh, in_specs=in_specs, out_specs=out_specs, check_vma=False)
```
